32 devices in a mesh: aux: 8 (over y, x, core), pair: 4 (over z).
Axes of the slice: x: 2, y: 2, z: 4, core: 2. Of those that a mesh axis runs over, the one named last changes fastest.
Arguments:
- b_slab: bfloat16 [8192, 8, 4096], P(('aux', 'pair')), may hold values from -6 to 6
- b_rows: bfloat16 [64, 8, 4096], P('aux', 'pair'), may hold values from -0.03125 to 0.03125
- g_occ: bfloat16 [512, 512], P(('aux', 'pair')), may hold values from -0.375 to 0.375
- g_virt: bfloat16 [512, 512], P(('aux', 'pair')), may hold values from -0.375 to 0.375
- pair_index: int32 [2, 8], replicated, may hold values from 0 to 7, as said below
Outputs:
- polar: float32 [8192, 64], P(('aux', 'pair'))
The draws below stay inside these ranges and needn't reach their ends.
Inputs may be any that keep to these rules, and one draw needn't show every extreme that they name: `pair_index`: no pair block repeats; every block index 0 to 7 is the first block of exactly 1 pair blocks.
All inputs are finite; a program needn't handle non-finite values.
Results may differ from the reference program's by a relative error of at most 0.004.
Values may be sent and summed in bfloat16 or wider, within the bound.
No kernel may reach another device: no remote copies, remote signals or barrier semaphores. Data moves between devices by JAX's collectives and lax.ppermute only.
A program may use at most 192 MiB of HBM per device.

```python
import jax
import jax.numpy as jnp
from jax import lax

BLK = 64
TILE = 4096
NB = 8
NAO = 512
NP = 8
SLAB = 8192
PROWS = 64


def draw_pair_index(key, part):
    key = jax.random.fold_in(key, 7)
    first_key, second_key = jax.random.split(key)
    row_order = jax.random.permutation(first_key, NB)
    shifts = jax.random.permutation(second_key, NB)
    slot_ids = jnp.arange(NP)
    first_block = row_order[slot_ids % NB]
    second_block = (first_block + shifts[slot_ids // NB]) % NB
    return jnp.stack([first_block, second_block]).astype(jnp.int32)


def levels(rng, shape, shards, smallest, top_value):
    def one(dim, blocks):
        heights = jax.random.uniform(jax.random.fold_in(jax.random.fold_in(rng, 6), dim), (blocks,), jnp.float32, smallest / len(shards), top_value / len(shards))
        return jnp.repeat(jnp.exp(heights), shape[dim] // blocks).reshape((-1,) + (1,) * (len(shape) - dim - 1))

    gain = one(*shards[0])
    for cut in shards[1:]:
        gain = gain * one(*cut)
    return gain


def normal_values(key, dims, scale, bound, shards=(), kind=jnp.bfloat16):
    gain = levels(key, dims, shards, -0.22, 0.18) if shards else 1.0
    values = jax.random.normal(key, dims, jnp.float32) * scale * gain
    return jnp.minimum(jnp.maximum(values, -bound), bound).astype(kind)


def setup_inputs(seed: int = 0) -> dict:
    key_of = jax.random.split(jax.random.key(seed), 6)
    b_slab = normal_values(key_of[0], (SLAB, NP, TILE), 1.0, 6.0, ((0, 32),))
    b_rows = normal_values(key_of[1], (PROWS, NP, TILE), (NP * TILE) ** -0.5, 0.03125, ((0, 8), (1, 4)))
    g_occ = normal_values(key_of[2], (NAO, NAO), (4 * BLK) ** -0.5, 0.375, ((0, 32),))
    g_virt = normal_values(key_of[3], (NAO, NAO), (4 * BLK) ** -0.5, 0.375, ((0, 32),))
    pair_index = draw_pair_index(jax.random.fold_in(key_of[5], 71), 0)
    return dict(b_slab=b_slab, b_rows=b_rows, g_occ=g_occ, g_virt=g_virt, pair_index=pair_index)


def block_tables(g_occ, g_virt, pair_index):
    first_block = pair_index[0]
    second_block = pair_index[1]
    occupied = g_occ.reshape(NB, BLK, NB, BLK)[first_block][:, :, first_block]
    virtual = g_virt.reshape(NB, BLK, NB, BLK)[second_block][:, :, second_block]
    return jnp.transpose(occupied, (2, 0, 1, 3)), jnp.transpose(virtual, (2, 0, 1, 3))


def project_slab(slab_rows, occ_tables, virt_tables):
    count = slab_rows.shape[0]
    pairs = slab_rows.shape[1]
    slab_tiles = jnp.moveaxis(slab_rows.reshape(count, pairs, BLK, BLK), 1, 0)

    def accumulate(running, inputs):
        occ_block, virt_block, tile_block = inputs
        half_step = jnp.einsum("kac,qcd->qkad", occ_block.astype(jnp.float32), tile_block.astype(jnp.float32)).astype(jnp.bfloat16)
        contrib = jnp.einsum("qkad,kbd->qkab", half_step.astype(jnp.float32), virt_block.astype(jnp.float32))
        return running + contrib, None

    start_value = jnp.zeros((count, pairs, BLK, BLK), jnp.float32)
    running, unused = lax.scan(accumulate, start_value, (occ_tables, virt_tables, slab_tiles))
    return running.astype(jnp.bfloat16).reshape(count, pairs * BLK * BLK)


def reference(b_slab, b_rows, g_occ, g_virt, pair_index):
    occ_tables, virt_tables = block_tables(g_occ, g_virt, pair_index)
    row_matrix = b_rows.reshape(PROWS, NP * TILE)
    group_rows = min(SLAB, 256)
    grouped = b_slab.reshape(SLAB // group_rows, group_rows, NP, TILE)

    def one_group(slab_rows):
        weighted = project_slab(slab_rows, occ_tables, virt_tables)
        return jnp.dot(weighted, row_matrix.T, preferred_element_type=jnp.float32)

    return lax.map(one_group, grouped).reshape(SLAB, PROWS)
```

```python
import functools

import jax
import jax.numpy as jnp
from jax import lax
from jax.experimental import pallas as pl
from jax.experimental.pallas import tpu as pltpu
from jax.sharding import PartitionSpec as P

BLK = 64
LANES = 128
PAIRS_HI = BLK * BLK // LANES
F32 = jnp.float32
BF16 = jnp.bfloat16
VMEM_LIMIT = 56 * 1024 * 1024


def swap(value, axis, size, offset):
    return lax.ppermute(value, axis, [(i, i ^ offset) for i in range(size)])


def dot(a, b, dims=(((1,), (0,)), ((), ())), precision=None):
    return lax.dot_general(a, b, dims, preferred_element_type=F32, precision=precision)


NT = (((1,), (1,)), ((), ()))


def tables_kernel(blocks, nz, *refs):
    g_refs = refs[: len(blocks)]
    row_id, occ_row, occ_col, virt_row, virt_col, occ_out, virt_out, occ_g, virt_g = refs[len(blocks) :]
    place = 0
    strip = g_refs[0].shape[2] // 8
    for ref in g_refs:
        for d in range(ref.shape[0]):
            for z in range(ref.shape[1]):
                for group in range(4):
                    base = group * 2 * strip
                    lanes = slice(group * LANES, (group + 1) * LANES)
                    occ_g[place : place + strip, lanes] = ref[d, z, base : base + strip, :]
                    virt_g[place : place + strip, lanes] = ref[d, z, base + strip : base + 2 * strip, :]
                place += strip
    rid = row_id[...]
    one = lambda hit: jnp.where(hit, 1.0, 0.0).astype(BF16)
    nao = occ_g.shape[1]
    picked = dot(one(occ_row[...] == rid), occ_g[...]).astype(BF16)
    col_rows = one(occ_col[...] == lax.broadcasted_iota(jnp.int32, (occ_col.shape[0], nao), 1))
    table = dot(col_rows, picked, NT).astype(BF16)
    half = table.shape[1] // 2
    for l in range(occ_out.shape[0]):
        for a_lo in range(2):
            occ_out[l, a_lo * BLK : (a_lo + 1) * BLK, :] = table[l * BLK : (l + 1) * BLK, a_lo * half : (a_lo + 1) * half]
    cols = one(lax.broadcasted_iota(jnp.int32, (nao, virt_col.shape[1]), 0) == virt_col[...])
    step = 4 * LANES
    for start in range(0, virt_row.shape[0], step):
        picked = dot(one(virt_row[start : start + step, :] == rid), virt_g[...]).astype(BF16)
        full = dot(picked, cols)
        same = (lax.broadcasted_iota(jnp.int32, full.shape, 0) // BLK) % 2 == (
            lax.broadcasted_iota(jnp.int32, full.shape, 1) // BLK
        ) % 2
        virt_out[start : start + step, :] = jnp.where(same, full, 0.0).astype(BF16)


def make_tables(g_blocks, row_id, m_rows, n_rows, m_cols, n_cols):
    nk, nl = m_rows.shape[0], m_cols.shape[0]
    nao = row_id.shape[0]
    ids = lambda *shape: lax.broadcasted_iota(jnp.int32, shape, len(shape) - 1)
    hi = jnp.arange(PAIRS_HI, dtype=jnp.int32) * 2
    lo = jnp.arange(2, dtype=jnp.int32)
    inner = jnp.arange(BLK, dtype=jnp.int32)
    occ_row = (m_rows[None, :, None] * BLK + hi[None, None, :] + lo[:, None, None]).reshape(-1, 1)
    occ_col = (m_cols[:, None, None] * BLK + hi[None, None, :] + lo[None, :, None]).reshape(-1, 1)
    virt_row = (n_rows[:, None, None] * BLK + 0 * lo[None, :, None] + inner[None, None, :]).reshape(-1, 1)
    virt_col = (n_cols[:, None, None] * BLK + 0 * lo[None, :, None] + inner[None, None, :]).reshape(1, -1)
    return pl.pallas_call(
        functools.partial(tables_kernel, g_blocks, None),
        out_shape=(
            jax.ShapeDtypeStruct((nl, 2 * BLK, nk * PAIRS_HI), BF16),
            jax.ShapeDtypeStruct((nk * LANES, nl * LANES), BF16),
        ),
        scratch_shapes=[pltpu.VMEM((nao, nao), BF16), pltpu.VMEM((nao, nao), BF16)],
        compiler_params=pltpu.CompilerParams(vmem_limit_bytes=VMEM_LIMIT),
        name="tables",
    )(*g_blocks, row_id.reshape(1, -1), occ_row, occ_col, virt_row, virt_col)


def transform_kernel(count, *refs):
    b_refs = refs[:count]
    virt, occ, out, x_buf, z_buf = refs[count:]
    nk = b_refs[0].shape[0]
    group = occ.shape[0]
    rows = b_refs[0].shape[1]
    per = rows // PAIRS_HI
    for k in range(nk):
        weights = virt[k * LANES : (k + 1) * LANES, :]
        for e in range(count):
            x = dot(b_refs[e][k], weights).astype(BF16)
            for l in range(group):
                for p in range(per):
                    x_buf[l, k * PAIRS_HI : (k + 1) * PAIRS_HI, (e * per + p) * LANES : (e * per + p + 1) * LANES] = x[
                        p * PAIRS_HI : (p + 1) * PAIRS_HI, l * LANES : (l + 1) * LANES
                    ]
    low = lax.broadcasted_iota(jnp.int32, (PAIRS_HI, LANES), 1) < BLK
    for l in range(group):
        y = dot(occ[l], x_buf[l])
        for p in range(count * per):
            part = y[:, p * LANES : (p + 1) * LANES]
            t0, t2, t1, t3 = (part[i * PAIRS_HI : (i + 1) * PAIRS_HI] for i in range(4))
            z_buf[p, :, :] = jnp.where(low, t0, t3) + pltpu.roll(jnp.where(low, t2, t1), BLK, 1)
        for c in range(PAIRS_HI):
            out[l, :, c * LANES : (c + 1) * LANES] = z_buf[:, c, :].astype(BF16)


def transform(b_blocks, occ, virt):
    nl, nk = occ.shape[0], b_blocks[0].shape[0]
    count = len(b_blocks)
    rows = b_blocks[0].shape[1]
    ps = count * rows // PAIRS_HI
    group = 4
    whole = pl.BlockSpec((nk, rows, LANES), lambda i: (0, 0, 0))
    return pl.pallas_call(
        functools.partial(transform_kernel, count),
        grid=(nl // group,),
        in_specs=[whole] * count
        + [
            pl.BlockSpec((nk * LANES, group * LANES), lambda i: (0, i)),
            pl.BlockSpec((group, 2 * BLK, nk * PAIRS_HI), lambda i: (i, 0, 0)),
        ],
        out_specs=pl.BlockSpec((group, ps, BLK * BLK), lambda i: (i, 0, 0)),
        out_shape=jax.ShapeDtypeStruct((nl, ps, BLK * BLK), BF16),
        scratch_shapes=[
            pltpu.VMEM((group, nk * PAIRS_HI, ps * LANES), BF16),
            pltpu.VMEM((ps, PAIRS_HI, LANES), F32),
        ],
        compiler_params=pltpu.CompilerParams(vmem_limit_bytes=VMEM_LIMIT),
        name="transform",
    )(*b_blocks, virt, occ)


def contract_kernel(pieces, nl, *refs):
    w_refs = refs[:pieces]
    slab, place, out, weights = refs[pieces:]

    @pl.when(pl.program_id(0) == 0)
    def _():
        for i, ref in enumerate(w_refs):
            n = ref.shape[0]
            weights[i * n : (i + 1) * n, :] = ref[...]

    full = dot(slab[...], weights[...], NT)
    per = w_refs[0].shape[0] // nl
    own = (lax.broadcasted_iota(jnp.int32, full.shape, 1) // per) % nl == lax.broadcasted_iota(
        jnp.int32, full.shape, 0
    ) % nl
    kept = jnp.where(own, full, 0.0).reshape(full.shape[0] // nl, nl, full.shape[1])
    summed = jnp.sum(kept, axis=1)
    out[...] = dot(summed, place[...], precision=lax.Precision.HIGHEST)


def contract(slab, w_pieces, place):
    count, nl, tile = slab.shape
    pieces = [w.reshape(-1, tile) for w in w_pieces]
    total = sum(w.shape[0] for w in pieces)
    rows = min(512, count * nl)
    fixed = lambda shape: pl.BlockSpec(shape, lambda i: (0, 0))
    return pl.pallas_call(
        functools.partial(contract_kernel, len(pieces), nl),
        grid=(count * nl // rows,),
        in_specs=[fixed(w.shape) for w in pieces]
        + [pl.BlockSpec((rows, tile), lambda i: (i, 0)), fixed(place.shape)],
        out_specs=pl.BlockSpec((rows // nl, place.shape[1]), lambda i: (i, 0)),
        out_shape=jax.ShapeDtypeStruct((count, place.shape[1]), F32),
        scratch_shapes=[pltpu.VMEM((total, tile), BF16)],
        compiler_params=pltpu.CompilerParams(vmem_limit_bytes=VMEM_LIMIT),
        name="contract",
    )(*pieces, slab.reshape(count * nl, tile), place)


def on_device(na, nz, b_slab, b_rows, g_occ, g_virt, pair_index):
    per, k_local, tile = b_rows.shape
    strip = g_occ.shape[0]
    nl = b_slab.shape[1]
    me_a, me_z = lax.axis_index("aux"), lax.axis_index("pair")
    outer = list(range(0, na, 2))

    b_own = jnp.transpose(b_rows.reshape(per, k_local, PAIRS_HI, LANES), (1, 0, 2, 3)).reshape(-1, LANES)
    g_own = jnp.concatenate([g_occ, g_virt], axis=0)
    g_own = jnp.concatenate([g_own[:, i * LANES : (i + 1) * LANES] for i in range(g_own.shape[1] // LANES)], axis=0)
    packed = jnp.concatenate([b_own, g_own], axis=0)
    column = [packed] + [swap(packed, "pair", nz, d) for d in range(1, nz)]
    b_z = jnp.concatenate([c[: b_own.shape[0]].reshape(k_local, per * PAIRS_HI, LANES) for c in column], axis=0)
    g_z = jnp.stack([c[b_own.shape[0] :] for c in column])

    g_half = jnp.stack([g_z] + [swap(g_z, "aux", na, e) for e in outer[1:]])
    g_other = swap(g_half, "aux", na, 1)
    b_blocks = [b_z]
    if len(outer) == 4:
        b_x, b_y = swap(b_z, "aux", na, 2), swap(b_z, "aux", na, 4)
        mid = b_z.shape[1] // 2
        diagonal = jnp.concatenate(
            [swap(b_x[:, :mid], "aux", na, 4), swap(b_y[:, mid:], "aux", na, 2)], axis=1
        )
        b_blocks += [b_x, b_y, diagonal]
    else:
        b_blocks += [swap(b_z, "aux", na, e) for e in outer[1:]]

    z_of = me_z ^ jnp.arange(nz, dtype=jnp.int32)
    aux_of = me_a ^ jnp.concatenate([jnp.asarray(outer, jnp.int32), jnp.asarray(outer, jnp.int32) + 1])
    row_id = ((aux_of[:, None] * nz + z_of[None, :])[:, :, None] * strip + jnp.arange(strip, dtype=jnp.int32)).reshape(-1)
    k_ids = (z_of[:, None] * k_local + jnp.arange(k_local, dtype=jnp.int32)).reshape(-1)
    first, second = pair_index[0], pair_index[1]
    occ, virt = make_tables([g_half, g_other], row_id, first[k_ids], second[k_ids], first, second)

    pieces = [transform(b_blocks[i : i + 2], occ, virt) for i in range(0, len(outer), 2)]
    others = [swap(w, "aux", na, 1) for w in pieces]

    core = jnp.arange(2, dtype=jnp.int32)[:, None, None, None, None]
    piece = jnp.arange(len(pieces), dtype=jnp.int32)[None, :, None, None, None]
    which = jnp.arange(2, dtype=jnp.int32)[None, None, None, :, None]
    row = jnp.arange(per, dtype=jnp.int32)
    target = (me_a ^ (piece * 4 + which * 2 + core)) * per + row
    target = jnp.broadcast_to(target, (2, len(pieces), nl, 2, per)).reshape(-1, 1)
    place = (target == jnp.arange(na * per, dtype=jnp.int32)).astype(F32)
    return contract(b_slab, pieces + others, place)


def solution(mesh):
    placed = (
        P(("aux", "pair"), None, None),
        P("aux", "pair", None),
        P(("aux", "pair"), None),
        P(("aux", "pair"), None),
        P(),
    )
    return jax.shard_map(
        functools.partial(on_device, mesh.shape["aux"], mesh.shape["pair"]),
        mesh=mesh,
        in_specs=placed,
        out_specs=P(("aux", "pair"), None),
        check_vma=False,
    )
```

```python
import functools

import jax
import jax.numpy as jnp
from jax import lax
from jax.experimental import pallas as pl
from jax.experimental.pallas import tpu as pltpu
from jax.sharding import PartitionSpec as P

BLK = 64
LANES = 128
HALF = BLK * BLK // LANES
F32 = jnp.float32
BF16 = jnp.bfloat16
MIB = 1024 * 1024
NT = (((1,), (1,)), ((), ()))
IN_VMEM = pl.BlockSpec(memory_space=pltpu.VMEM)
IN_PLACE = pl.BlockSpec(memory_space=pl.ANY)
IN_SMEM = pl.BlockSpec(memory_space=pltpu.SMEM)


def swap(value, axis, size, offset):
    return lax.ppermute(value, axis, [(i, i ^ offset) for i in range(size)])


def dot(a, b, dims=(((1,), (0,)), ((), ())), precision=None):
    return lax.dot_general(a, b, dims, preferred_element_type=F32, precision=precision)


def iota(shape, dim):
    return lax.broadcasted_iota(jnp.int32, shape, dim)


def in_hbm(value):
    return pltpu.with_memory_space_constraint(value, pltpu.HBM)


def hot(hit):
    return jnp.where(hit, 1.0, 0.0).astype(BF16)


def tables_body(nz, k_local, me, pair, g_refs, occ_out, virt_out, occ_g, virt_g, pick, cols, wide):
    strip = g_refs[0].shape[1] // 8
    nao = occ_g.shape[0]
    nl = occ_out.shape[0]
    nk = virt_out.shape[0] // LANES
    place = 0
    for ref in g_refs:
        for z in range(ref.shape[0]):
            for group in range(4):
                base = group * 2 * strip
                lanes = slice(group * LANES, (group + 1) * LANES)
                occ_g[place : place + strip, lanes] = ref[z, base : base + strip, :]
                virt_g[place : place + strip, lanes] = ref[z, base + strip : base + 2 * strip, :]
            place += strip
    at = iota((1, nao), 1)
    block = at // (nz * strip)
    half = nao // (nz * strip) // 2
    offset = 2 * (block % half) + block // half
    held = (((me[0] ^ offset) * nz) + (me[1] ^ (at // strip) % nz)) * strip + at % strip
    lane = iota((1, nao), 1)
    k_of = [(me[1] ^ (k // k_local)) * k_local + k % k_local for k in range(nk)]

    for k in range(nk):
        for lo in range(2):
            row = pair[0, k_of[k]] * BLK + 2 * iota((HALF, 1), 0) + lo
            pick[(lo * nk + k) * HALF : (lo * nk + k + 1) * HALF, :] = hot(row == held)
    picked = dot(pick[...], occ_g[...]).astype(BF16)
    for l in range(nl):
        for lo in range(2):
            col = pair[0, l] * BLK + 2 * iota((HALF, 1), 0) + lo
            cols[(2 * l + lo) * HALF : (2 * l + lo + 1) * HALF, :] = hot(col == lane)
    table = dot(cols[...], picked, NT).astype(BF16)
    side = nk * HALF
    for l in range(nl):
        for lo in range(2):
            occ_out[l, lo * BLK : (lo + 1) * BLK, :] = table[l * BLK : (l + 1) * BLK, lo * side : (lo + 1) * side]

    for k in range(nk):
        row = pair[1, k_of[k]] * BLK + iota((BLK, 1), 0)
        pick[k * BLK : (k + 1) * BLK, :] = hot(row == held)
    picked = dot(pick[...], virt_g[...]).astype(BF16)
    for l in range(nl):
        col = pair[1, l] * BLK + iota((1, LANES), 1) % BLK
        wide[:, l * LANES : (l + 1) * LANES] = hot(iota((nao, 1), 0) == col)
    full = dot(picked, wide[...])
    for k in range(nk):
        part = full[k * BLK : (k + 1) * BLK, :]
        low = (iota(part.shape, 1) // BLK) % 2 == 0
        virt_out[k * LANES : k * LANES + BLK, :] = jnp.where(low, part, 0.0).astype(BF16)
        virt_out[k * LANES + BLK : (k + 1) * LANES, :] = jnp.where(low, 0.0, part).astype(BF16)


def tables_kernel(count, nz, k_local, me, pair, *refs):
    tables_body(nz, k_local, me, pair, refs[:count], *refs[count:])


def tables_shapes(nao, nl):
    out = (
        jax.ShapeDtypeStruct((nl, 2 * BLK, nl * HALF), BF16),
        jax.ShapeDtypeStruct((nl * LANES, nl * LANES), BF16),
    )
    scratch = [
        pltpu.VMEM((nao, nao), BF16),
        pltpu.VMEM((nao, nao), BF16),
        pltpu.VMEM((nl * BLK, nao), BF16),
        pltpu.VMEM((nl * BLK, nao), BF16),
        pltpu.VMEM((nao, nl * LANES), BF16),
    ]
    return out, scratch


def make_tables(g_blocks, me, pair_index, nz, k_local):
    nl = pair_index.shape[1]
    nao = len(g_blocks) * g_blocks[0].shape[0] * (g_blocks[0].shape[1] // 8)
    out, scratch = tables_shapes(nao, nl)
    return pl.pallas_call(
        functools.partial(tables_kernel, len(g_blocks), nz, k_local),
        in_specs=[IN_SMEM, IN_SMEM] + [IN_VMEM] * len(g_blocks),
        out_specs=[IN_VMEM, IN_VMEM],
        out_shape=out,
        scratch_shapes=scratch,
        compiler_params=pltpu.CompilerParams(vmem_limit_bytes=24 * MIB),
        name="tables",
    )(me, pair_index, *g_blocks)


def transform_body(blocks, rows, virt, occ, out, done, x_buf, z_buf):
    nl = occ.shape[0]
    count = len(blocks)
    per = rows // HALF
    for e in range(count):
        k = 0
        for ref, length in blocks[e]:
            for j in range(length):
                held = ref[j] if len(ref.shape) == 3 else ref[j * rows : (j + 1) * rows, :]
                for l in range(0, nl, 2):
                    weights = virt[k * LANES : (k + 1) * LANES, l * LANES : (l + 2) * LANES]
                    x = dot(held, weights).astype(BF16)
                    for i in range(2):
                        for p in range(per):
                            at = (e * per + p) * LANES
                            x_buf[l + i, k * HALF : (k + 1) * HALF, at : at + LANES] = x[
                                p * HALF : (p + 1) * HALF, i * LANES : (i + 1) * LANES
                            ]
                k += 1
    low = iota((HALF, LANES), 1) < BLK
    for l in range(nl):
        y = dot(occ[l], x_buf[l])
        for p in range(count * per):
            part = y[:, p * LANES : (p + 1) * LANES]
            t0, t2, t1, t3 = (part[i * HALF : (i + 1) * HALF] for i in range(4))
            z = jnp.where(low, t0, t3) + pltpu.roll(jnp.where(low, t2, t1), BLK, 1)
            z_buf[p, :, :] = z.astype(BF16)
        turned = jnp.swapaxes(z_buf[...], 0, 1)
        for c in range(HALF):
            out[l, done : done + count * per, c * LANES : (c + 1) * LANES] = turned[c]


def runs_of(layout, refs):
    refs = iter(refs)
    return [[(next(refs), length) for length in block] for block in layout]


def transform_kernel(layout, rows, *refs):
    total = sum(map(len, layout))
    virt, occ = refs[total : total + 2]
    out, x_buf, z_buf = refs[-3:]
    done = 0
    for before in refs[total + 2 : -3]:
        done = before.shape[1]
        out[:, :done, :] = before[...]
    transform_body(runs_of(layout, refs[:total]), rows, virt, occ, out, done, x_buf, z_buf)


def whole_block(value):
    return pl.BlockSpec(value.shape, lambda i: (0,) * len(value.shape))


def transform(blocks, rows, occ, virt, before=()):
    nl = occ.shape[0]
    layout = [[length for _, length in block] for block in blocks]
    flat = [run for block in blocks for run, _ in block]
    ps = len(blocks) * rows // HALF
    held = ps + sum(b.shape[1] for b in before)
    group = nl if nl <= 8 else 4
    return pl.pallas_call(
        functools.partial(transform_kernel, layout, rows),
        grid=(nl // group,),
        in_specs=[whole_block(run) for run in flat]
        + [
            pl.BlockSpec((nl * LANES, group * LANES), lambda i: (0, i)),
            pl.BlockSpec((group, 2 * BLK, nl * HALF), lambda i: (i, 0, 0)),
        ]
        + [pl.BlockSpec((group,) + b.shape[1:], lambda i: (i, 0, 0)) for b in before],
        out_specs=pl.BlockSpec((group, held, BLK * BLK), lambda i: (i, 0, 0)),
        out_shape=jax.ShapeDtypeStruct((nl, held, BLK * BLK), BF16),
        scratch_shapes=[
            pltpu.VMEM((group, nl * HALF, ps * LANES), BF16),
            pltpu.VMEM((ps, HALF, LANES), BF16),
        ],
        compiler_params=pltpu.CompilerParams(vmem_limit_bytes=36 * MIB),
        name="transform",
    )(*flat, virt, occ, *before)


def prepare_kernel(layout, rows, count, after, nz, k_local, me, pair, *refs):
    g_refs, refs = refs[:count], refs[count:]
    total = sum(map(len, layout))
    runs, refs = refs[:total], refs[total + after :]
    occ, virt, out = refs[:3]
    tables_body(nz, k_local, me, pair, g_refs, occ, virt, *refs[3:8])
    transform_body(runs_of(layout, runs), rows, virt, occ, out, 0, *refs[8:])


def prepare(g_blocks, blocks, rows, me, pair_index, nz, k_local, after):
    nl = pair_index.shape[1]
    nao = len(g_blocks) * g_blocks[0].shape[0] * (g_blocks[0].shape[1] // 8)
    out, scratch = tables_shapes(nao, nl)
    layout = [[length for _, length in block] for block in blocks]
    flat = [run for block in blocks for run, _ in block]
    ps = len(blocks) * rows // HALF
    return pl.pallas_call(
        functools.partial(prepare_kernel, layout, rows, len(g_blocks), len(after), nz, k_local),
        in_specs=[IN_SMEM, IN_SMEM] + [IN_VMEM] * (len(g_blocks) + len(flat)) + [IN_PLACE] * len(after),
        out_specs=[IN_VMEM] * 3,
        out_shape=out + (jax.ShapeDtypeStruct((nl, ps, BLK * BLK), BF16),),
        scratch_shapes=scratch
        + [pltpu.VMEM((nl, nl * HALF, ps * LANES), BF16), pltpu.VMEM((ps, HALF, LANES), BF16)],
        compiler_params=pltpu.CompilerParams(vmem_limit_bytes=44 * MIB),
        name="prepare",
    )(me, pair_index, *g_blocks, *flat, *map(in_hbm, after))


def reorder_kernel(slab, out):
    q, nl, tile = slab.shape
    n = q * nl
    row, col = iota((n, n), 0), iota((n, n), 1)
    order = hot((row % q) * nl + row // q == col)
    step = 512
    for t in range(0, tile, step):
        moved = dot(order, slab[:, :, t : t + step].reshape(n, step)).astype(BF16)
        for l in range(nl):
            out[l, :, t : t + step] = moved[l * q : (l + 1) * q]


def reorder(slab, part, parts):
    count, nl, tile = slab.shape
    q = 256 // nl
    steps = count // parts // q
    return pl.pallas_call(
        reorder_kernel,
        grid=(steps,),
        in_specs=[pl.BlockSpec((q, nl, tile), lambda i: (part * steps + i, 0, 0))],
        out_specs=pl.BlockSpec((nl, q, tile), lambda i: (0, i, 0)),
        out_shape=pltpu.HBM((nl, count // parts, tile), BF16),
        compiler_params=pltpu.CompilerParams(vmem_limit_bytes=24 * MIB),
        name="reorder",
    )(in_hbm(slab))


def stack_kernel(split, nz, after, *refs):
    refs, b_out, g_out = refs[: -2 - after], refs[-2], refs[-1]
    column, side = refs[: nz - 1], refs[nz - 1 :]
    k_local = b_out.shape[0] // len(column)
    rows = split // k_local
    for i, ref in enumerate(column):
        for j in range(k_local):
            b_out[i * k_local + j] = ref[j * rows : (j + 1) * rows, :]
    for i, ref in enumerate(side):
        g_out[i] = ref[split:, :]


def stack(column, side, split, k_local, after):
    one = column[0].shape[0] - split
    return pl.pallas_call(
        functools.partial(stack_kernel, split, len(column) + 1, len(after)),
        in_specs=[IN_VMEM] * (len(column) + len(side)) + [IN_PLACE] * len(after),
        out_specs=[IN_VMEM, IN_VMEM],
        out_shape=(
            jax.ShapeDtypeStruct((len(column) * k_local, split // k_local, LANES), BF16),
            jax.ShapeDtypeStruct((len(side), one, LANES), BF16),
        ),
        compiler_params=pltpu.CompilerParams(vmem_limit_bytes=8 * MIB),
        name="stack",
    )(*column, *side, *map(in_hbm, after))


def collect_kernel(split, nz, sides, *refs):
    near, side, far, out = refs[:nz], refs[nz : nz + sides], refs[nz + sides : 2 * nz + sides - 1], refs[-1]
    for z, ref in enumerate(near):
        out[z] = ref[split:, :]
    for e, ref in enumerate(side):
        out[(e + 1) * nz] = ref[split:, :]
        for z, block in enumerate(far):
            out[(e + 1) * nz + z + 1] = block[e]


def collect(own, column, side, far, split, after):
    nz = len(column) + 1
    return pl.pallas_call(
        functools.partial(collect_kernel, split, nz, len(side)),
        in_specs=[IN_VMEM] * (nz + len(side) + len(far)) + [IN_PLACE] * len(after),
        out_specs=IN_VMEM,
        out_shape=jax.ShapeDtypeStruct((nz * (len(side) + 1), own.shape[0] - split, LANES), BF16),
        compiler_params=pltpu.CompilerParams(vmem_limit_bytes=8 * MIB),
        name="collect",
    )(own, *column, *side, *far, *map(in_hbm, after))


def contract_kernel(parts, place, *refs):
    slabs, w_refs, out, total = refs[:parts], refs[parts:-2], refs[-2], refs[-1]
    l = pl.program_id(0)
    weights = jnp.concatenate([w[0] for w in w_refs], axis=0)
    count = slabs[0].shape[1]

    @pl.when(l == 0)
    def _():
        total[...] = jnp.zeros_like(total)

    for i, slab in enumerate(slabs):
        total[i * count : (i + 1) * count, :] += dot(slab[0], weights, NT)

    @pl.when(l == pl.num_programs(0) - 1)
    def _():
        out[...] = dot(place[...], total[...], NT, precision=lax.Precision.HIGHEST)


def contract(slabs, w_pieces, place):
    nl, count, tile = slabs[0].shape
    rows = place.shape[0]
    count *= len(slabs)
    one = lambda value: pl.BlockSpec((1,) + value.shape[1:], lambda i: (i, 0, 0))
    return pl.pallas_call(
        functools.partial(contract_kernel, len(slabs)),
        grid=(nl,),
        in_specs=[whole_block(place)] + [one(s) for s in slabs] + [one(w) for w in w_pieces],
        out_specs=pl.BlockSpec((rows, count), lambda i: (0, 0)),
        out_shape=jax.ShapeDtypeStruct((rows, count), F32),
        scratch_shapes=[pltpu.VMEM((count, rows), F32)],
        compiler_params=pltpu.CompilerParams(vmem_limit_bytes=28 * MIB),
        name="contract",
    )(place, *map(in_hbm, slabs), *w_pieces)


def on_device(na, nz, b_slab, b_rows, g_occ, g_virt, pair_index):
    per, k_local, tile = b_rows.shape
    me_a, me_z = lax.axis_index("aux"), lax.axis_index("pair")
    me = jnp.stack([me_a, me_z]).astype(jnp.int32)
    outer = list(range(0, na, 2))
    rows = per * HALF
    split = k_local * rows

    g_own = jnp.concatenate([g_occ, g_virt], axis=0)
    b_own = jnp.transpose(b_rows.reshape(per, k_local, HALF, LANES), (1, 0, 2, 3)).reshape(-1, LANES)
    own = jnp.concatenate([b_own] + [g_own[:, i : i + LANES] for i in range(0, g_own.shape[1], LANES)], axis=0)

    column = [swap(own, "pair", nz, d) for d in range(1, nz)]
    side = [swap(own, "aux", na, e) for e in outer[1:]]
    slabs = [reorder(b_slab, 0, 2)]
    b_z, g_side = stack(column, side, split, k_local, slabs)

    b_z, b_slab = lax.optimization_barrier((b_z, b_slab))
    slabs.append(reorder(b_slab, 1, 2))
    far = [[(swap(b_z, "aux", na, e), b_z.shape[0])] for e in outer[1 : 3 if len(outer) == 4 else None]]
    g_far = [swap(g_side, "pair", nz, d) for d in range(1, nz)]
    if len(outer) == 4:
        cut = b_z.shape[0] // 2
        low, high = far[0][0][0][:cut], far[1][0][0][cut:]
        far.append([(swap(low, "aux", na, 4), cut), (swap(high, "aux", na, 2), b_z.shape[0] - cut)])
    g_half = collect(own, column, side, g_far, split, slabs[1:])
    g_blocks = [g_half, swap(g_half, "aux", na, 1)]
    blocks = [[(own, k_local), (b_z, b_z.shape[0])]] + [[(b, k_local)] + f for b, f in zip(side, far)]
    if len(outer) == 4:
        occ, virt, first = prepare(g_blocks, blocks[:3], rows, me, pair_index, nz, k_local, slabs)
        pieces = [transform(blocks[3:], rows, occ, virt, [first])]
    else:
        occ, virt = make_tables(g_blocks, me, pair_index, nz, k_local)
        pieces = [transform(blocks[i : i + 2], rows, occ, virt) for i in range(0, len(outer), 2)]
    others = [swap(w, "aux", na, 1) for w in pieces]

    count = na * per
    at = jnp.arange(count, dtype=jnp.int32)
    block = at // per
    target = (me_a ^ (2 * (block % (na // 2)) + block // (na // 2))) * per + at % per
    place = (target[None, :] == at[:, None]).astype(F32)
    return contract(slabs, pieces + others, place).T


def solution(mesh):
    placed = (
        P(("aux", "pair"), None, None),
        P("aux", "pair", None),
        P(("aux", "pair"), None),
        P(("aux", "pair"), None),
        P(),
    )
    return jax.shard_map(
        functools.partial(on_device, mesh.shape["aux"], mesh.shape["pair"]),
        mesh=mesh,
        in_specs=placed,
        out_specs=P(("aux", "pair"), None),
        check_vma=False,
    )
```

```python
import functools

import jax
import jax.numpy as jnp
from jax import lax
from jax.experimental import pallas as pl
from jax.experimental.pallas import tpu as pltpu
from jax.sharding import PartitionSpec as P

BLK = 64
LANES = 128
HALF = BLK * BLK // LANES
F32 = jnp.float32
BF16 = jnp.bfloat16
MIB = 1024 * 1024
NT = (((1,), (1,)), ((), ()))
IN_VMEM = pl.BlockSpec(memory_space=pltpu.VMEM)
IN_PLACE = pl.BlockSpec(memory_space=pl.ANY)
IN_SMEM = pl.BlockSpec(memory_space=pltpu.SMEM)


def swap(value, axis, size, offset):
    return lax.ppermute(value, axis, [(i, i ^ offset) for i in range(size)])


def dot(a, b, dims=(((1,), (0,)), ((), ())), precision=None):
    return lax.dot_general(a, b, dims, preferred_element_type=F32, precision=precision)


def iota(shape, dim):
    return lax.broadcasted_iota(jnp.int32, shape, dim)


def in_hbm(value):
    return pltpu.with_memory_space_constraint(value, pltpu.HBM)


def in_vmem(value):
    return pltpu.with_memory_space_constraint(value, pltpu.VMEM)


def hot(hit):
    return jnp.where(hit, 1.0, 0.0).astype(BF16)


def tables_body(nz, k_local, me, pair, g_refs, occ_out, virt_out, occ_g, virt_g, pick, cols, wide):
    strip = g_refs[0].shape[1] // 8
    nao = occ_g.shape[0]
    nl = occ_out.shape[0]
    nk = virt_out.shape[0] // LANES
    place = 0
    for ref in g_refs:
        for z in range(ref.shape[0]):
            for group in range(4):
                base = group * 2 * strip
                lanes = slice(group * LANES, (group + 1) * LANES)
                occ_g[place : place + strip, lanes] = ref[z, base : base + strip, :]
                virt_g[place : place + strip, lanes] = ref[z, base + strip : base + 2 * strip, :]
            place += strip
    at = iota((1, nao), 1)
    block = at // (nz * strip)
    half = nao // (nz * strip) // 2
    offset = 2 * (block % half) + block // half
    held = (((me[0] ^ offset) * nz) + (me[1] ^ (at // strip) % nz)) * strip + at % strip
    lane = iota((1, nao), 1)
    k_of = [(me[1] ^ (k // k_local)) * k_local + k % k_local for k in range(nk)]

    for k in range(nk):
        for lo in range(2):
            row = pair[0, k_of[k]] * BLK + 2 * iota((HALF, 1), 0) + lo
            pick[(lo * nk + k) * HALF : (lo * nk + k + 1) * HALF, :] = hot(row == held)
    picked = dot(pick[...], occ_g[...]).astype(BF16)
    for l in range(nl):
        for lo in range(2):
            col = pair[0, l] * BLK + 2 * iota((HALF, 1), 0) + lo
            cols[(2 * l + lo) * HALF : (2 * l + lo + 1) * HALF, :] = hot(col == lane)
    table = dot(cols[...], picked, NT).astype(BF16)
    side = nk * HALF
    for l in range(nl):
        for lo in range(2):
            occ_out[l, lo * BLK : (lo + 1) * BLK, :] = table[l * BLK : (l + 1) * BLK, lo * side : (lo + 1) * side]

    for k in range(nk):
        row = pair[1, k_of[k]] * BLK + iota((BLK, 1), 0)
        pick[k * BLK : (k + 1) * BLK, :] = hot(row == held)
    picked = dot(pick[...], virt_g[...]).astype(BF16)
    for l in range(nl):
        col = pair[1, l] * BLK + iota((1, LANES), 1) % BLK
        wide[:, l * LANES : (l + 1) * LANES] = hot(iota((nao, 1), 0) == col)
    full = dot(picked, wide[...])
    for k in range(nk):
        part = full[k * BLK : (k + 1) * BLK, :]
        low = (iota(part.shape, 1) // BLK) % 2 == 0
        virt_out[k * LANES : k * LANES + BLK, :] = jnp.where(low, part, 0.0).astype(BF16)
        virt_out[k * LANES + BLK : (k + 1) * LANES, :] = jnp.where(low, 0.0, part).astype(BF16)


def tables_kernel(count, nz, k_local, me, pair, *refs):
    tables_body(nz, k_local, me, pair, refs[:count], *refs[count:])


def tables_shapes(nao, nl):
    out = (
        jax.ShapeDtypeStruct((nl, 2 * BLK, nl * HALF), BF16),
        jax.ShapeDtypeStruct((nl * LANES, nl * LANES), BF16),
    )
    scratch = [
        pltpu.VMEM((nao, nao), BF16),
        pltpu.VMEM((nao, nao), BF16),
        pltpu.VMEM((nl * BLK, nao), BF16),
        pltpu.VMEM((nl * BLK, nao), BF16),
        pltpu.VMEM((nao, nl * LANES), BF16),
    ]
    return out, scratch


def make_tables(g_blocks, me, pair_index, nz, k_local):
    nl = pair_index.shape[1]
    nao = len(g_blocks) * g_blocks[0].shape[0] * (g_blocks[0].shape[1] // 8)
    out, scratch = tables_shapes(nao, nl)
    return pl.pallas_call(
        functools.partial(tables_kernel, len(g_blocks), nz, k_local),
        in_specs=[IN_SMEM, IN_SMEM] + [IN_VMEM] * len(g_blocks),
        out_specs=[IN_VMEM, IN_VMEM],
        out_shape=out,
        scratch_shapes=scratch,
        compiler_params=pltpu.CompilerParams(vmem_limit_bytes=24 * MIB),
        name="tables",
    )(me, pair_index, *g_blocks)


def transform_body(blocks, rows, virt, occ, out, done, x_buf, z_buf):
    nl = occ.shape[0]
    count = len(blocks)
    per = rows // HALF
    for e in range(count):
        k = 0
        for ref, length in blocks[e]:
            for j in range(length):
                held = ref[j] if len(ref.shape) == 3 else ref[j * rows : (j + 1) * rows, :]
                for l in range(0, nl, 2):
                    weights = virt[k * LANES : (k + 1) * LANES, l * LANES : (l + 2) * LANES]
                    x = dot(held, weights).astype(BF16)
                    for i in range(2):
                        for p in range(per):
                            at = (e * per + p) * LANES
                            x_buf[l + i, k * HALF : (k + 1) * HALF, at : at + LANES] = x[
                                p * HALF : (p + 1) * HALF, i * LANES : (i + 1) * LANES
                            ]
                k += 1
    low = iota((HALF, LANES), 1) < BLK
    for l in range(nl):
        y = dot(occ[l], x_buf[l])
        for p in range(count * per):
            part = y[:, p * LANES : (p + 1) * LANES]
            t0, t2, t1, t3 = (part[i * HALF : (i + 1) * HALF] for i in range(4))
            z = jnp.where(low, t0, t3) + pltpu.roll(jnp.where(low, t2, t1), BLK, 1)
            z_buf[p, :, :] = z.astype(BF16)
        turned = jnp.swapaxes(z_buf[...], 0, 1)
        for c in range(HALF):
            out[l, done : done + count * per, c * LANES : (c + 1) * LANES] = turned[c]


def runs_of(layout, refs):
    refs = iter(refs)
    return [[(next(refs), length) for length in block] for block in layout]


def transform_kernel(layout, rows, *refs):
    total = sum(map(len, layout))
    virt, occ = refs[total : total + 2]
    out, x_buf, z_buf = refs[-3:]
    done = 0
    for before in refs[total + 2 : -3]:
        done = before.shape[1]
        out[:, :done, :] = before[...]
    transform_body(runs_of(layout, refs[:total]), rows, virt, occ, out, done, x_buf, z_buf)


def whole_block(value):
    return pl.BlockSpec(value.shape, lambda i: (0,) * len(value.shape))


def transform(blocks, rows, occ, virt, before=()):
    nl = occ.shape[0]
    layout = [[length for _, length in block] for block in blocks]
    flat = [run for block in blocks for run, _ in block]
    ps = len(blocks) * rows // HALF
    held = ps + sum(b.shape[1] for b in before)
    group = nl if nl <= 8 else 4
    return pl.pallas_call(
        functools.partial(transform_kernel, layout, rows),
        grid=(nl // group,),
        in_specs=[whole_block(run) for run in flat]
        + [
            pl.BlockSpec((nl * LANES, group * LANES), lambda i: (0, i)),
            pl.BlockSpec((group, 2 * BLK, nl * HALF), lambda i: (i, 0, 0)),
        ]
        + [pl.BlockSpec((group,) + b.shape[1:], lambda i: (i, 0, 0)) for b in before],
        out_specs=pl.BlockSpec((group, held, BLK * BLK), lambda i: (i, 0, 0)),
        out_shape=jax.ShapeDtypeStruct((nl, held, BLK * BLK), BF16),
        scratch_shapes=[
            pltpu.VMEM((group, nl * HALF, ps * LANES), BF16),
            pltpu.VMEM((ps, HALF, LANES), BF16),
        ],
        compiler_params=pltpu.CompilerParams(vmem_limit_bytes=(18 if nl <= 8 else 36) * MIB),
        name="transform",
    )(*flat, virt, occ, *before)


def prepare_kernel(layout, rows, count, after, nz, k_local, me, pair, *refs):
    g_refs, refs = refs[:count], refs[count:]
    total = sum(map(len, layout))
    runs, refs = refs[:total], refs[total + after :]
    occ, virt, out = refs[:3]
    tables_body(nz, k_local, me, pair, g_refs, occ, virt, *refs[3:8])
    transform_body(runs_of(layout, runs), rows, virt, occ, out, 0, *refs[8:])


def prepare(g_blocks, blocks, rows, me, pair_index, nz, k_local, after):
    nl = pair_index.shape[1]
    nao = len(g_blocks) * g_blocks[0].shape[0] * (g_blocks[0].shape[1] // 8)
    out, scratch = tables_shapes(nao, nl)
    layout = [[length for _, length in block] for block in blocks]
    flat = [run for block in blocks for run, _ in block]
    ps = len(blocks) * rows // HALF
    return pl.pallas_call(
        functools.partial(prepare_kernel, layout, rows, len(g_blocks), len(after), nz, k_local),
        in_specs=[IN_SMEM, IN_SMEM] + [IN_VMEM] * (len(g_blocks) + len(flat)) + [IN_PLACE] * len(after),
        out_specs=[IN_VMEM] * 3,
        out_shape=out + (jax.ShapeDtypeStruct((nl, ps, BLK * BLK), BF16),),
        scratch_shapes=scratch
        + [pltpu.VMEM((nl, nl * HALF, ps * LANES), BF16), pltpu.VMEM((ps, HALF, LANES), BF16)],
        compiler_params=pltpu.CompilerParams(vmem_limit_bytes=27 * MIB),
        name="prepare",
    )(me, pair_index, *g_blocks, *flat, *after)


def reorder_kernel(slab, out):
    q, nl, tile = slab.shape
    at = 0 if out.shape[1] == q else pl.multiple_of(pl.program_id(0) * q, q)
    n = q * nl
    row, col = iota((n, n), 0), iota((n, n), 1)
    order = hot((row % q) * nl + row // q == col)
    step = 512
    for t in range(0, tile, step):
        moved = dot(order, slab[:, :, t : t + step].reshape(n, step)).astype(BF16)
        for l in range(nl):
            out[l, pl.ds(at, q), t : t + step] = moved[l * q : (l + 1) * q]


def reorder(slab, first, last, parts, space):
    count, nl, tile = slab.shape
    q = 256 // nl
    skip = count * first // parts // q
    steps = count * last // parts // q - skip
    return pl.pallas_call(
        reorder_kernel,
        grid=(steps,),
        in_specs=[pl.BlockSpec((q, nl, tile), lambda i: (skip + i, 0, 0))],
        out_specs=IN_VMEM if space == pltpu.VMEM else pl.BlockSpec((nl, q, tile), lambda i: (0, i, 0)),
        out_shape=space((nl, steps * q, tile), BF16),
        compiler_params=pltpu.CompilerParams(vmem_limit_bytes=24 * MIB),
        name="reorder",
    )(in_hbm(slab))


def pack_kernel(b_in, occ_in, virt_in, out, b_rows, g_occ, g_virt, sems):
    moves = [
        pltpu.make_async_copy(source, to, sems.at[i])
        for i, (source, to) in enumerate(((b_in, b_rows), (occ_in, g_occ), (virt_in, g_virt)))
    ]
    for move in moves:
        move.start()
    for move in moves:
        move.wait()
    per, k_local, _ = b_rows.shape
    for k in range(k_local):
        held = b_rows[:, k, :].astype(F32)
        for p in range(per):
            out[(k * per + p) * HALF : (k * per + p + 1) * HALF, :] = held[p].reshape(HALF, LANES).astype(BF16)
    at = k_local * per * HALF
    strip = g_occ.shape[0]
    for i in range(0, g_occ.shape[1], LANES):
        for ref in (g_occ, g_virt):
            out[at : at + strip, :] = ref[:, i : i + LANES]
            at += strip


def pack(b_rows, g_occ, g_virt):
    total = (b_rows.size + 2 * g_occ.size) // LANES
    return pl.pallas_call(
        pack_kernel,
        in_specs=[IN_PLACE] * 3,
        out_specs=IN_VMEM,
        out_shape=jax.ShapeDtypeStruct((total, LANES), BF16),
        scratch_shapes=[pltpu.VMEM(x.shape, BF16) for x in (b_rows, g_occ, g_virt)] + [pltpu.SemaphoreType.DMA((3,))],
        compiler_params=pltpu.CompilerParams(vmem_limit_bytes=8 * MIB),
        name="pack",
    )(in_hbm(b_rows), in_hbm(g_occ), in_hbm(g_virt))


def stack_kernel(split, nz, after, *refs):
    refs, b_out, g_out = refs[: -2 - after], refs[-2], refs[-1]
    column, side = refs[: nz - 1], refs[nz - 1 :]
    k_local = b_out.shape[0] // len(column)
    rows = split // k_local
    for i, ref in enumerate(column):
        for j in range(k_local):
            b_out[i * k_local + j] = ref[j * rows : (j + 1) * rows, :]
    for i, ref in enumerate(side):
        g_out[i] = ref[split:, :]


def stack(column, side, split, k_local, after):
    one = column[0].shape[0] - split
    return pl.pallas_call(
        functools.partial(stack_kernel, split, len(column) + 1, len(after)),
        in_specs=[IN_VMEM] * (len(column) + len(side)) + [IN_PLACE] * len(after),
        out_specs=[IN_VMEM, IN_VMEM],
        out_shape=(
            jax.ShapeDtypeStruct((len(column) * k_local, split // k_local, LANES), BF16),
            jax.ShapeDtypeStruct((len(side), one, LANES), BF16),
        ),
        compiler_params=pltpu.CompilerParams(vmem_limit_bytes=8 * MIB),
        name="stack",
    )(*column, *side, *after)


def collect_kernel(split, nz, sides, *refs):
    near, side, far, out = refs[:nz], refs[nz : nz + sides], refs[nz + sides : 2 * nz + sides - 1], refs[-1]
    for z, ref in enumerate(near):
        out[z] = ref[split:, :]
    for e, ref in enumerate(side):
        out[(e + 1) * nz] = ref[split:, :]
        for z, block in enumerate(far):
            out[(e + 1) * nz + z + 1] = block[e]


def collect(own, column, side, far, split, after):
    nz = len(column) + 1
    return pl.pallas_call(
        functools.partial(collect_kernel, split, nz, len(side)),
        in_specs=[IN_VMEM] * (nz + len(side) + len(far)) + [IN_PLACE] * len(after),
        out_specs=IN_VMEM,
        out_shape=jax.ShapeDtypeStruct((nz * (len(side) + 1), own.shape[0] - split, LANES), BF16),
        compiler_params=pltpu.CompilerParams(vmem_limit_bytes=8 * MIB),
        name="collect",
    )(own, *column, *side, *far, *after)


def contract_kernel(parts, place, *refs):
    slabs, w_refs, out = refs[:parts], refs[parts:-1], refs[-1]
    total = [None] * parts
    for l in range(slabs[0].shape[0]):
        weights = jnp.concatenate([w[l] for w in w_refs], axis=0)
        for i, slab in enumerate(slabs):
            part = dot(slab[l], weights, NT)
            total[i] = part if total[i] is None else total[i] + part
    total = jnp.concatenate(total, axis=0)
    out[...] = dot(place[...], total, NT, precision=lax.Precision.HIGHEST)


def contract(slabs, w_pieces, place):
    parts = len(slabs)
    return pl.pallas_call(
        functools.partial(contract_kernel, parts),
        in_specs=[IN_VMEM] * (1 + parts + len(w_pieces)),
        out_specs=IN_VMEM,
        out_shape=jax.ShapeDtypeStruct((place.shape[0], sum(slab.shape[1] for slab in slabs)), F32),
        compiler_params=pltpu.CompilerParams(vmem_limit_bytes=28 * MIB),
        name="contract",
    )(place, *map(in_vmem, slabs), *w_pieces)


def on_device(na, nz, b_slab, b_rows, g_occ, g_virt, pair_index):
    per, k_local, tile = b_rows.shape
    me_a, me_z = lax.axis_index("aux"), lax.axis_index("pair")
    me = jnp.stack([me_a, me_z]).astype(jnp.int32)
    outer = list(range(0, na, 2))
    rows = per * HALF
    split = k_local * rows

    own = pack(b_rows, g_occ, g_virt)

    side = [swap(own, "aux", na, e) for e in outer[1:]]
    column = [swap(own, "pair", nz, d) for d in range(1, nz)]
    slabs = [reorder(b_slab, 0, 2, 4, pltpu.HBM)]
    b_z, g_side = stack(column, side, split, k_local, [in_hbm(slabs[0])])

    b_z, b_slab = lax.optimization_barrier((b_z, b_slab))
    slabs.append(reorder(b_slab, 2, 3, 4, pltpu.HBM))
    g_far = [swap(g_side, "pair", nz, d) for d in range(1, nz)]
    far = [[(swap(b_z, "aux", na, e), b_z.shape[0])] for e in outer[1 : 3 if len(outer) == 4 else None]]
    if len(outer) == 4:
        cut = b_z.shape[0] // 2
        low, high = far[0][0][0][:cut], far[1][0][0][cut:]
        far.append([(swap(low, "aux", na, 4), cut), (swap(high, "aux", na, 2), b_z.shape[0] - cut)])
    close = [block[0][0] for block in far[:2]]
    g_half = collect(own, column, side, g_far, split, [in_hbm(slabs[1])] + (close if len(outer) == 4 else []))
    g_blocks = [g_half, swap(g_half, "aux", na, 1)]
    blocks = [[(own, k_local), (b_z, b_z.shape[0])]] + [[(b, k_local)] + f for b, f in zip(side, far)]
    if len(outer) == 4:
        occ, virt, first = prepare(g_blocks, blocks[:3], rows, me, pair_index, nz, k_local, [])
        pieces = [transform(blocks[3:], rows, occ, virt, [first])]
    else:
        occ, virt = make_tables(g_blocks, me, pair_index, nz, k_local)
        pieces = [transform(blocks[i : i + 2], rows, occ, virt) for i in range(0, len(outer), 2)]
    pieces[-1], b_slab = lax.optimization_barrier((pieces[-1], b_slab))
    others = [swap(w, "aux", na, 1) for w in pieces]

    count = na * per
    at = jnp.arange(count, dtype=jnp.int32)
    block = at // per
    target = (me_a ^ (2 * (block % (na // 2)) + block // (na // 2))) * per + at % per
    place = (target[None, :] == at[:, None]).astype(F32)
    slabs.append(reorder(b_slab, 3, 4, 4, pltpu.VMEM))
    return contract(slabs, pieces + others, place).T


def solution(mesh):
    placed = (
        P(("aux", "pair"), None, None),
        P("aux", "pair", None),
        P(("aux", "pair"), None),
        P(("aux", "pair"), None),
        P(),
    )
    return jax.shard_map(
        functools.partial(on_device, mesh.shape["aux"], mesh.shape["pair"]),
        mesh=mesh,
        in_specs=placed,
        out_specs=P(("aux", "pair"), None),
        check_vma=False,
    )
```

```python
import functools

import jax
import jax.numpy as jnp
from jax import lax
from jax.experimental import pallas as pl
from jax.experimental.pallas import tpu as pltpu
from jax.sharding import PartitionSpec as P

BLK = 64
LANES = 128
HALF = BLK * BLK // LANES
F32 = jnp.float32
BF16 = jnp.bfloat16
MIB = 1024 * 1024
PAD = 16
NT = (((1,), (1,)), ((), ()))
IN_VMEM = pl.BlockSpec(memory_space=pltpu.VMEM)
IN_PLACE = pl.BlockSpec(memory_space=pl.ANY)
IN_SMEM = pl.BlockSpec(memory_space=pltpu.SMEM)


def swap(value, axis, size, offset):
    return lax.ppermute(value, axis, [(i, i ^ offset) for i in range(size)])


def dot(a, b, dims=(((1,), (0,)), ((), ())), precision=None):
    return lax.dot_general(a, b, dims, preferred_element_type=F32, precision=precision)


def iota(shape, dim):
    return lax.broadcasted_iota(jnp.int32, shape, dim)


def in_hbm(value):
    return pltpu.with_memory_space_constraint(value, pltpu.HBM)


def in_vmem(value):
    return pltpu.with_memory_space_constraint(value, pltpu.VMEM)


def hot(hit):
    return jnp.where(hit, 1.0, 0.0).astype(BF16)


def tables_body(nz, k_local, me, pair, g_refs, occ_out, virt_out, occ_g, virt_g, pick, cols, wide):
    strip = g_refs[0].shape[1] // 8
    nao = occ_g.shape[0]
    nl = occ_out.shape[0]
    nk = virt_out.shape[0] // LANES
    place = 0
    for ref in g_refs:
        for z in range(ref.shape[0]):
            at = place
            if strip % 16 == 0:
                e, c = divmod(place // (nz * strip), nao // (nz * strip) // 2)
                at = ((me[0] ^ (2 * c + e)) * nz + (me[1] ^ (z % nz))) * strip
                at = pl.multiple_of(at, strip)
            for group in range(4):
                base = group * 2 * strip
                lanes = slice(group * LANES, (group + 1) * LANES)
                occ_g[place : place + strip, lanes] = ref[z, base : base + strip, :]
                virt_g[pl.ds(at, strip), lanes] = ref[z, base + strip : base + 2 * strip, :]
            place += strip
    at = iota((1, nao), 1)
    block = at // (nz * strip)
    half = nao // (nz * strip) // 2
    offset = 2 * (block % half) + block // half
    held = (((me[0] ^ offset) * nz) + (me[1] ^ (at // strip) % nz)) * strip + at % strip
    lane = iota((1, nao), 1)
    k_of = [(me[1] ^ (k // k_local)) * k_local + k % k_local for k in range(nk)]

    for k in range(nk):
        for lo in range(2):
            row = pair[0, k_of[k]] * BLK + 2 * iota((HALF, 1), 0) + lo
            pick[(lo * nk + k) * HALF : (lo * nk + k + 1) * HALF, :] = hot(row == held)
    picked = dot(pick[...], occ_g[...]).astype(BF16)
    for l in range(nl):
        for lo in range(2):
            col = pair[0, l] * BLK + 2 * iota((HALF, 1), 0) + lo
            cols[(2 * l + lo) * HALF : (2 * l + lo + 1) * HALF, :] = hot(col == lane)
    table = dot(cols[...], picked, NT).astype(BF16)
    side = nk * HALF
    for l in range(nl):
        for lo in range(2):
            occ_out[l, lo * BLK : (lo + 1) * BLK, :] = table[l * BLK : (l + 1) * BLK, lo * side : (lo + 1) * side]

    side = iota((1, LANES), 1) // BLK
    low = jnp.bitwise_and(iota((1, nl * LANES), 1), BLK) == 0
    keep = [hot(low), hot(jnp.logical_not(low))]
    if strip % 16 == 0:
        for l in range(nl):
            block = pair[1, l]
            group = pl.multiple_of((block // 2) * LANES, LANES)
            part = virt_g[:, pl.ds(group, LANES)].astype(F32)
            wide[:, l * LANES : (l + 1) * LANES] = jnp.where(
                side == block % 2, part, pltpu.roll(part, BLK, 1)
            ).astype(BF16)
        for k in range(nk):
            part = wide[pl.ds(pl.multiple_of(pair[1, k_of[k]] * BLK, BLK), BLK), :]
            for lo in range(2):
                virt_out[k * LANES + lo * BLK : k * LANES + (lo + 1) * BLK, :] = part * keep[lo]
        return
    for k in range(nk):
        row = pair[1, k_of[k]] * BLK + iota((BLK, 1), 0)
        pick[k * BLK : (k + 1) * BLK, :] = hot(row == held)
    picked = dot(pick[...], virt_g[...]).astype(BF16)
    for l in range(nl):
        col = pair[1, l] * BLK + iota((1, LANES), 1) % BLK
        wide[:, l * LANES : (l + 1) * LANES] = hot(iota((nao, 1), 0) == col)
    full = dot(picked, wide[...])
    for k in range(nk):
        part = full[k * BLK : (k + 1) * BLK, :]
        low = jnp.bitwise_and(iota(part.shape, 1), BLK) == 0
        virt_out[k * LANES : k * LANES + BLK, :] = jnp.where(low, part, 0.0).astype(BF16)
        virt_out[k * LANES + BLK : (k + 1) * LANES, :] = jnp.where(low, 0.0, part).astype(BF16)


def tables_kernel(count, nz, k_local, me, pair, *refs):
    tables_body(nz, k_local, me, pair, refs[:count], *refs[count:])


def tables_shapes(nao, nl):
    out = (
        jax.ShapeDtypeStruct((nl, 2 * BLK, nl * HALF), BF16),
        jax.ShapeDtypeStruct((nl * LANES, nl * LANES), BF16),
    )
    scratch = [
        pltpu.VMEM((nao, nao), BF16),
        pltpu.VMEM((nao, nao), BF16),
        pltpu.VMEM((nl * BLK, nao), BF16),
        pltpu.VMEM((nl * BLK, nao), BF16),
        pltpu.VMEM((nao, nl * LANES), BF16),
    ]
    return out, scratch


def make_tables(g_blocks, me, pair_index, nz, k_local):
    nl = pair_index.shape[1]
    nao = len(g_blocks) * g_blocks[0].shape[0] * (g_blocks[0].shape[1] // 8)
    out, scratch = tables_shapes(nao, nl)
    return pl.pallas_call(
        functools.partial(tables_kernel, len(g_blocks), nz, k_local),
        in_specs=[IN_SMEM, IN_SMEM] + [IN_VMEM] * len(g_blocks),
        out_specs=[IN_VMEM, IN_VMEM],
        out_shape=out,
        scratch_shapes=scratch,
        compiler_params=pltpu.CompilerParams(vmem_limit_bytes=24 * MIB),
        name="tables",
    )(me, pair_index, *g_blocks)


def transform_body(blocks, rows, virt, occ, out, done, x_buf, z_buf):
    nl = occ.shape[0]
    count = len(blocks)
    per = rows // HALF
    held = []
    for block in blocks:
        held.append([])
        for ref, length in block:
            held[-1] += [(ref, j) for j in range(length)]
    for k in range(len(held[0])):
        block_rows = [
            ref[j] if len(ref.shape) == 3 else ref[j * rows : (j + 1) * rows, :] for ref, j in (h[k] for h in held)
        ]
        block_rows = jnp.concatenate(block_rows, axis=0) if count > 1 else block_rows[0]
        for l in range(0, nl, 2):
            weights = virt[k * LANES : (k + 1) * LANES, l * LANES : (l + 2) * LANES]
            x = dot(block_rows, weights).astype(BF16)
            for i in range(2):
                for p in range(count * per):
                    x_buf[l + i, k * HALF : (k + 1) * HALF, p * LANES : (p + 1) * LANES] = x[
                        p * HALF : (p + 1) * HALF, i * LANES : (i + 1) * LANES
                    ]
    low = iota((HALF, LANES), 1) < BLK
    for l in range(nl):
        y = dot(occ[l], x_buf[l])
        for p in range(count * per):
            part = y[:, p * LANES : (p + 1) * LANES]
            t0, t2, t1, t3 = (part[i * HALF : (i + 1) * HALF] for i in range(4))
            z = jnp.where(low, t0, t3) + pltpu.roll(jnp.where(low, t2, t1), BLK, 1)
            z_buf[p, :, :] = z.astype(BF16)
        turned = jnp.swapaxes(z_buf[...], 0, 1)
        for c in range(HALF):
            out[l, done : done + count * per, c * LANES : (c + 1) * LANES] = turned[c]


def runs_of(layout, refs):
    refs = iter(refs)
    return [[(next(refs), length) for length in block] for block in layout]


def transform_kernel(layout, rows, *refs):
    total = sum(map(len, layout))
    virt, occ = refs[total : total + 2]
    out, x_buf, z_buf = refs[-3:]
    done = 0
    for before in refs[total + 2 : -3]:
        done = before.shape[1]
        out[:, :done, :] = before[...]
    transform_body(runs_of(layout, refs[:total]), rows, virt, occ, out, done, x_buf, z_buf)


def whole_block(value):
    return pl.BlockSpec(value.shape, lambda i: (0,) * len(value.shape))


def transform(blocks, rows, occ, virt, before=()):
    nl = occ.shape[0]
    layout = [[length for _, length in block] for block in blocks]
    flat = [run for block in blocks for run, _ in block]
    ps = len(blocks) * rows // HALF
    held = ps + sum(b.shape[1] for b in before)
    group = nl if nl <= 8 else 4
    return pl.pallas_call(
        functools.partial(transform_kernel, layout, rows),
        grid=(nl // group,),
        in_specs=[whole_block(run) for run in flat]
        + [
            pl.BlockSpec((nl * LANES, group * LANES), lambda i: (0, i)),
            pl.BlockSpec((group, 2 * BLK, nl * HALF), lambda i: (i, 0, 0)),
        ]
        + [pl.BlockSpec((group,) + b.shape[1:], lambda i: (i, 0, 0)) for b in before],
        out_specs=pl.BlockSpec((group, held, BLK * BLK), lambda i: (i, 0, 0)),
        out_shape=jax.ShapeDtypeStruct((nl, held, BLK * BLK), BF16),
        scratch_shapes=[
            pltpu.VMEM((group, nl * HALF, ps * LANES), BF16),
            pltpu.VMEM((ps, HALF, LANES), BF16),
        ],
        compiler_params=pltpu.CompilerParams(vmem_limit_bytes=(18 if nl <= 8 else 36) * MIB),
        name="transform",
    )(*flat, virt, occ, *before)


def prepare_kernel(layout, rows, count, after, nz, k_local, me, pair, *refs):
    g_refs, refs = refs[:count], refs[count:]
    total = sum(map(len, layout))
    runs, refs = refs[:total], refs[total + after :]
    occ, virt, out = refs[:3]
    tables_body(nz, k_local, me, pair, g_refs, occ, virt, *refs[3:8])
    transform_body(runs_of(layout, runs), rows, virt, occ, out, 0, *refs[8:])


def prepare(g_blocks, blocks, rows, me, pair_index, nz, k_local, after):
    nl = pair_index.shape[1]
    nao = len(g_blocks) * g_blocks[0].shape[0] * (g_blocks[0].shape[1] // 8)
    out, scratch = tables_shapes(nao, nl)
    layout = [[length for _, length in block] for block in blocks]
    flat = [run for block in blocks for run, _ in block]
    ps = len(blocks) * rows // HALF
    return pl.pallas_call(
        functools.partial(prepare_kernel, layout, rows, len(g_blocks), len(after), nz, k_local),
        in_specs=[IN_SMEM, IN_SMEM] + [IN_VMEM] * (len(g_blocks) + len(flat)) + [IN_PLACE] * len(after),
        out_specs=[IN_VMEM] * 3,
        out_shape=out + (jax.ShapeDtypeStruct((nl, ps, BLK * BLK), BF16),),
        scratch_shapes=scratch
        + [pltpu.VMEM((nl, nl * HALF, ps * LANES), BF16), pltpu.VMEM((ps, HALF, LANES), BF16)],
        compiler_params=pltpu.CompilerParams(vmem_limit_bytes=27 * MIB),
        name="prepare",
    )(me, pair_index, *g_blocks, *flat, *after)


def reorder_kernel(slab, out, order):
    q, nl, tile = slab.shape
    n = q * nl

    @pl.when(pl.program_id(0) == 0)
    def _():
        for l in range(nl):
            order[l * q : (l + 1) * q, :] = hot(iota((q, n), 1) == iota((q, n), 0) * nl + l)

    at = 0 if out.shape[1] == q else pl.multiple_of(pl.program_id(0) * q, q)
    step = 512
    for t in range(0, tile, step):
        moved = dot(order[...], slab[:, :, t : t + step].reshape(n, step)).astype(BF16)
        for l in range(nl):
            out[l, pl.ds(at, q), t : t + step] = moved[l * q : (l + 1) * q]


def reorder(slab, first, last, parts, space):
    count, nl, tile = slab.shape
    q = 256 // nl
    skip = count * first // parts // q
    steps = count * last // parts // q - skip
    return pl.pallas_call(
        reorder_kernel,
        grid=(steps,),
        in_specs=[pl.BlockSpec((q, nl, tile), lambda i: (skip + i, 0, 0))],
        out_specs=IN_VMEM if space == pltpu.VMEM else pl.BlockSpec((nl, q, tile), lambda i: (0, i, 0)),
        out_shape=space((nl, steps * q, tile), BF16),
        scratch_shapes=[pltpu.VMEM((q * nl, q * nl), BF16)],
        compiler_params=pltpu.CompilerParams(vmem_limit_bytes=16 * MIB),
        name="reorder",
    )(in_hbm(slab))


def pack_kernel(b_in, occ_in, virt_in, out, padded, b_rows, g_occ, g_virt, sems):
    moves = [
        pltpu.make_async_copy(source, to, sems.at[i])
        for i, (source, to) in enumerate(((b_in, b_rows), (occ_in, g_occ), (virt_in, g_virt)))
    ]
    for move in moves:
        move.start()
    for move in moves:
        move.wait()
    per, k_local, _ = b_rows.shape
    for k in range(k_local):
        held = b_rows[:, k, :].astype(F32)
        for p in range(per):
            out[(k * per + p) * HALF : (k * per + p + 1) * HALF, :] = held[p].reshape(HALF, LANES).astype(BF16)
    at = k_local * per * HALF
    strip = g_occ.shape[0]
    for i in range(0, g_occ.shape[1], LANES):
        for ref in (g_occ, g_virt):
            out[at : at + strip, :] = ref[:, i : i + LANES]
            at += strip
    padded[:at, :] = out[...]
    padded[at:, :] = jnp.zeros_like(padded[at:, :])


def pack(b_rows, g_occ, g_virt):
    total = (b_rows.size + 2 * g_occ.size) // LANES
    return pl.pallas_call(
        pack_kernel,
        in_specs=[IN_PLACE] * 3,
        out_specs=[IN_VMEM, IN_VMEM],
        out_shape=(jax.ShapeDtypeStruct((total, LANES), BF16), jax.ShapeDtypeStruct((total + PAD, LANES), BF16)),
        scratch_shapes=[pltpu.VMEM(x.shape, BF16) for x in (b_rows, g_occ, g_virt)] + [pltpu.SemaphoreType.DMA((3,))],
        compiler_params=pltpu.CompilerParams(vmem_limit_bytes=8 * MIB),
        name="pack",
    )(in_hbm(b_rows), in_hbm(g_occ), in_hbm(g_virt))


def stack_kernel(split, nz, after, *refs):
    refs, b_out, g_out = refs[: -2 - after], refs[-2], refs[-1]
    column, side = refs[: nz - 1], refs[nz - 1 :]
    k_local = b_out.shape[0] // len(column)
    rows = split // k_local
    for i, ref in enumerate(column):
        for j in range(k_local):
            b_out[i * k_local + j] = ref[j * rows : (j + 1) * rows, :]
    for i, ref in enumerate(side):
        g_out[i] = ref[split:, :]


def stack(column, side, split, k_local, after):
    one = side[0].shape[0] - split
    return pl.pallas_call(
        functools.partial(stack_kernel, split, len(column) + 1, len(after)),
        in_specs=[IN_VMEM] * (len(column) + len(side)) + [IN_PLACE] * len(after),
        out_specs=[IN_VMEM, IN_VMEM],
        out_shape=(
            jax.ShapeDtypeStruct((len(column) * k_local, split // k_local, LANES), BF16),
            jax.ShapeDtypeStruct((len(side), one, LANES), BF16),
        ),
        compiler_params=pltpu.CompilerParams(vmem_limit_bytes=8 * MIB),
        name="stack",
    )(*column, *side, *after)


def collect_kernel(split, nz, sides, *refs):
    near, side, far, out = refs[:nz], refs[nz : nz + sides], refs[nz + sides : 2 * nz + sides - 1], refs[-1]
    for z, ref in enumerate(near):
        out[z] = ref[split : split + out.shape[1], :]
    for e, ref in enumerate(side):
        out[(e + 1) * nz] = ref[split:, :]
        for z, block in enumerate(far):
            out[(e + 1) * nz + z + 1] = block[e]


def collect(own, column, side, far, split, after):
    nz = len(column) + 1
    return pl.pallas_call(
        functools.partial(collect_kernel, split, nz, len(side)),
        in_specs=[IN_VMEM] * (nz + len(side) + len(far)) + [IN_PLACE] * len(after),
        out_specs=IN_VMEM,
        out_shape=jax.ShapeDtypeStruct((nz * (len(side) + 1), own.shape[0] - split, LANES), BF16),
        compiler_params=pltpu.CompilerParams(vmem_limit_bytes=8 * MIB),
        name="collect",
    )(own, *column, *side, *far, *after)


def contract_kernel(parts, place, *refs):
    slabs, w_refs, out = refs[:parts], refs[parts:-1], refs[-1]
    total = [None] * parts
    for l in range(slabs[0].shape[0]):
        weights = jnp.concatenate([w[l] for w in w_refs], axis=0)
        for i, slab in enumerate(slabs):
            part = dot(slab[l], weights, NT)
            total[i] = part if total[i] is None else total[i] + part
    total = jnp.concatenate(total, axis=0)
    out[...] = dot(place[...], total, NT, precision=lax.Precision.HIGHEST)


def contract(slabs, w_pieces, place):
    parts = len(slabs)
    return pl.pallas_call(
        functools.partial(contract_kernel, parts),
        in_specs=[IN_VMEM] * (1 + parts + len(w_pieces)),
        out_specs=IN_VMEM,
        out_shape=jax.ShapeDtypeStruct((place.shape[0], sum(slab.shape[1] for slab in slabs)), F32),
        compiler_params=pltpu.CompilerParams(vmem_limit_bytes=28 * MIB),
        name="contract",
    )(place, *map(in_vmem, slabs), *w_pieces)


def on_device(na, nz, b_slab, b_rows, g_occ, g_virt, pair_index):
    per, k_local, tile = b_rows.shape
    me_a, me_z = lax.axis_index("aux"), lax.axis_index("pair")
    me = jnp.stack([me_a, me_z]).astype(jnp.int32)
    outer = list(range(0, na, 2))
    rows = per * HALF
    split = k_local * rows

    own, padded = pack(b_rows, g_occ, g_virt)

    side = [swap(own, "aux", na, e) for e in outer[1:]]
    column = [swap(padded, "pair", nz, d) for d in range(1, nz)]
    slabs = [reorder(b_slab, 0, 2, 4, pltpu.HBM)]
    b_z, g_side = stack(column, side, split, k_local, [in_hbm(slabs[0])])

    b_z, b_slab = lax.optimization_barrier((b_z, b_slab))
    slabs.append(reorder(b_slab, 2, 3, 4, pltpu.HBM))
    g_far = [swap(g_side, "pair", nz, d) for d in range(1, nz)]
    far = [[(swap(b_z, "aux", na, e), b_z.shape[0])] for e in outer[1 : 3 if len(outer) == 4 else None]]
    if len(outer) == 4:
        cut = b_z.shape[0] // 2
        low, high = far[0][0][0][:cut], far[1][0][0][cut:]
        far.append([(swap(low, "aux", na, 4), cut), (swap(high, "aux", na, 2), b_z.shape[0] - cut)])
    close = [block[0][0] for block in far[:2]]
    g_half = collect(own, column, side, g_far, split, [in_hbm(slabs[1])] + (close if len(outer) == 4 else []))
    g_blocks = [g_half, swap(g_half, "aux", na, 1)]
    blocks = [[(own, k_local), (b_z, b_z.shape[0])]] + [[(b, k_local)] + f for b, f in zip(side, far)]
    if len(outer) == 4:
        occ, virt, first = prepare(g_blocks, blocks[:3], rows, me, pair_index, nz, k_local, [])
        pieces = [transform(blocks[3:], rows, occ, virt, [first])]
    else:
        occ, virt = make_tables(g_blocks, me, pair_index, nz, k_local)
        pieces = [transform(blocks[i : i + 2], rows, occ, virt) for i in range(0, len(outer), 2)]
    pieces[-1], b_slab = lax.optimization_barrier((pieces[-1], b_slab))
    others = [swap(w, "aux", na, 1) for w in pieces]

    count = na * per
    at = jnp.arange(count, dtype=jnp.int32)
    block = at // per
    target = (me_a ^ (2 * (block % (na // 2)) + block // (na // 2))) * per + at % per
    place = (target[None, :] == at[:, None]).astype(F32)
    slabs.append(reorder(b_slab, 3, 4, 4, pltpu.VMEM))
    return contract(slabs, pieces + others, place).T


def solution(mesh):
    placed = (
        P(("aux", "pair"), None, None),
        P("aux", "pair", None),
        P(("aux", "pair"), None),
        P(("aux", "pair"), None),
        P(),
    )
    return jax.shard_map(
        functools.partial(on_device, mesh.shape["aux"], mesh.shape["pair"]),
        mesh=mesh,
        in_specs=placed,
        out_specs=P(("aux", "pair"), None),
        check_vma=False,
    )
```

```python
import functools

import jax
import jax.numpy as jnp
from jax import lax
from jax.experimental import pallas as pl
from jax.experimental.pallas import tpu as pltpu
from jax.sharding import PartitionSpec as P

BLK = 64
LANES = 128
HALF = BLK * BLK // LANES
F32 = jnp.float32
BF16 = jnp.bfloat16
MIB = 1024 * 1024
PAD = 16
NT = (((1,), (1,)), ((), ()))
IN_VMEM = pl.BlockSpec(memory_space=pltpu.VMEM)
IN_PLACE = pl.BlockSpec(memory_space=pl.ANY)
IN_SMEM = pl.BlockSpec(memory_space=pltpu.SMEM)


def swap(value, axis, size, offset):
    return lax.ppermute(value, axis, [(i, i ^ offset) for i in range(size)])


def dot(a, b, dims=(((1,), (0,)), ((), ())), precision=None):
    return lax.dot_general(a, b, dims, preferred_element_type=F32, precision=precision)


def iota(shape, dim):
    return lax.broadcasted_iota(jnp.int32, shape, dim)


def in_hbm(value):
    return pltpu.with_memory_space_constraint(value, pltpu.HBM)


def in_vmem(value):
    return pltpu.with_memory_space_constraint(value, pltpu.VMEM)


def hot(hit):
    return jnp.where(hit, 1.0, 0.0).astype(BF16)


def tables_body(nz, k_local, me, pair, g_refs, occ_out, virt_out, occ_g, virt_g, pick, cols, wide):
    strip = g_refs[0].shape[1] // 8
    nao = occ_g.shape[0]
    nl = occ_out.shape[0]
    nk = virt_out.shape[0] // LANES
    place = 0
    for ref in g_refs:
        for z in range(ref.shape[0]):
            at = place
            if strip % 16 == 0:
                e, c = divmod(place // (nz * strip), nao // (nz * strip) // 2)
                at = ((me[0] ^ (2 * c + e)) * nz + (me[1] ^ (z % nz))) * strip
                at = pl.multiple_of(at, strip)
            for group in range(4):
                base = group * 2 * strip
                lanes = slice(group * LANES, (group + 1) * LANES)
                occ_g[place : place + strip, lanes] = ref[z, base : base + strip, :]
                virt_g[pl.ds(at, strip), lanes] = ref[z, base + strip : base + 2 * strip, :]
            place += strip
    at = iota((1, nao), 1)
    block = at // (nz * strip)
    half = nao // (nz * strip) // 2
    offset = 2 * (block % half) + block // half
    held = (((me[0] ^ offset) * nz) + (me[1] ^ (at // strip) % nz)) * strip + at % strip
    lane = iota((1, nao), 1)
    k_of = [(me[1] ^ (k // k_local)) * k_local + k % k_local for k in range(nk)]

    for k in range(nk):
        for lo in range(2):
            row = pair[0, k_of[k]] * BLK + 2 * iota((HALF, 1), 0) + lo
            pick[(lo * nk + k) * HALF : (lo * nk + k + 1) * HALF, :] = hot(row == held)
    picked = dot(pick[...], occ_g[...]).astype(BF16)
    for l in range(nl):
        for lo in range(2):
            col = pair[0, l] * BLK + 2 * iota((HALF, 1), 0) + lo
            cols[(2 * l + lo) * HALF : (2 * l + lo + 1) * HALF, :] = hot(col == lane)
    table = dot(cols[...], picked, NT).astype(BF16)
    side = nk * HALF
    for l in range(nl):
        for lo in range(2):
            occ_out[l, lo * BLK : (lo + 1) * BLK, :] = table[l * BLK : (l + 1) * BLK, lo * side : (lo + 1) * side]

    side = iota((1, LANES), 1) // BLK
    low = jnp.bitwise_and(iota((1, nl * LANES), 1), BLK) == 0
    keep = [hot(low), hot(jnp.logical_not(low))]
    if strip % 16 == 0:
        for l in range(nl):
            block = pair[1, l]
            group = pl.multiple_of((block // 2) * LANES, LANES)
            part = virt_g[:, pl.ds(group, LANES)].astype(F32)
            wide[:, l * LANES : (l + 1) * LANES] = jnp.where(
                side == block % 2, part, pltpu.roll(part, BLK, 1)
            ).astype(BF16)
        for k in range(nk):
            part = wide[pl.ds(pl.multiple_of(pair[1, k_of[k]] * BLK, BLK), BLK), :]
            for lo in range(2):
                virt_out[k * LANES + lo * BLK : k * LANES + (lo + 1) * BLK, :] = part * keep[lo]
        return
    for k in range(nk):
        row = pair[1, k_of[k]] * BLK + iota((BLK, 1), 0)
        pick[k * BLK : (k + 1) * BLK, :] = hot(row == held)
    picked = dot(pick[...], virt_g[...]).astype(BF16)
    for l in range(nl):
        col = pair[1, l] * BLK + iota((1, LANES), 1) % BLK
        wide[:, l * LANES : (l + 1) * LANES] = hot(iota((nao, 1), 0) == col)
    full = dot(picked, wide[...])
    for k in range(nk):
        part = full[k * BLK : (k + 1) * BLK, :]
        low = jnp.bitwise_and(iota(part.shape, 1), BLK) == 0
        virt_out[k * LANES : k * LANES + BLK, :] = jnp.where(low, part, 0.0).astype(BF16)
        virt_out[k * LANES + BLK : (k + 1) * LANES, :] = jnp.where(low, 0.0, part).astype(BF16)


def tables_kernel(count, nz, k_local, me, pair, *refs):
    tables_body(nz, k_local, me, pair, refs[:count], *refs[count:])


def tables_shapes(nao, nl):
    out = (
        jax.ShapeDtypeStruct((nl, 2 * BLK, nl * HALF), BF16),
        jax.ShapeDtypeStruct((nl * LANES, nl * LANES), BF16),
    )
    scratch = [
        pltpu.VMEM((nao, nao), BF16),
        pltpu.VMEM((nao, nao), BF16),
        pltpu.VMEM((nl * BLK, nao), BF16),
        pltpu.VMEM((nl * BLK, nao), BF16),
        pltpu.VMEM((nao, nl * LANES), BF16),
    ]
    return out, scratch


def make_tables(g_blocks, me, pair_index, nz, k_local):
    nl = pair_index.shape[1]
    nao = len(g_blocks) * g_blocks[0].shape[0] * (g_blocks[0].shape[1] // 8)
    out, scratch = tables_shapes(nao, nl)
    return pl.pallas_call(
        functools.partial(tables_kernel, len(g_blocks), nz, k_local),
        in_specs=[IN_SMEM, IN_SMEM] + [IN_VMEM] * len(g_blocks),
        out_specs=[IN_VMEM, IN_VMEM],
        out_shape=out,
        scratch_shapes=scratch,
        compiler_params=pltpu.CompilerParams(vmem_limit_bytes=24 * MIB),
        name="tables",
    )(me, pair_index, *g_blocks)


def transform_body(blocks, rows, virt, occ, out, done, x_buf, z_buf):
    nl = occ.shape[0]
    count = len(blocks)
    per = rows // HALF
    held = []
    for block in blocks:
        held.append([])
        for ref, length in block:
            held[-1] += [(ref, j) for j in range(length)]
    for k in range(len(held[0])):
        block_rows = [
            ref[j] if len(ref.shape) == 3 else ref[j * rows : (j + 1) * rows, :] for ref, j in (h[k] for h in held)
        ]
        block_rows = jnp.concatenate(block_rows, axis=0) if count > 1 else block_rows[0]
        for l in range(0, nl, 2):
            weights = virt[k * LANES : (k + 1) * LANES, l * LANES : (l + 2) * LANES]
            x = dot(block_rows, weights).astype(BF16)
            for i in range(2):
                for p in range(count * per):
                    x_buf[l + i, k * HALF : (k + 1) * HALF, p * LANES : (p + 1) * LANES] = x[
                        p * HALF : (p + 1) * HALF, i * LANES : (i + 1) * LANES
                    ]
    low = iota((HALF, LANES), 1) < BLK
    for l in range(nl):
        y = dot(occ[l], x_buf[l])
        for p in range(count * per):
            part = y[:, p * LANES : (p + 1) * LANES]
            t0, t2, t1, t3 = (part[i * HALF : (i + 1) * HALF] for i in range(4))
            z = jnp.where(low, t0, t3) + pltpu.roll(jnp.where(low, t2, t1), BLK, 1)
            z_buf[p, :, :] = z.astype(BF16)
        turned = jnp.swapaxes(z_buf[...], 0, 1)
        for c in range(HALF):
            out[l, done : done + count * per, c * LANES : (c + 1) * LANES] = turned[c]


def runs_of(layout, refs):
    refs = iter(refs)
    return [[(next(refs), length) for length in block] for block in layout]


def transform_kernel(layout, rows, *refs):
    total = sum(map(len, layout))
    virt, occ = refs[total : total + 2]
    out, x_buf, z_buf = refs[-3:]
    done = 0
    for before in refs[total + 2 : -3]:
        done = before.shape[1]
        out[:, :done, :] = before[...]
    transform_body(runs_of(layout, refs[:total]), rows, virt, occ, out, done, x_buf, z_buf)


def whole_block(value):
    return pl.BlockSpec(value.shape, lambda i: (0,) * len(value.shape))


def transform(blocks, rows, occ, virt, before=()):
    nl = occ.shape[0]
    layout = [[length for _, length in block] for block in blocks]
    flat = [run for block in blocks for run, _ in block]
    ps = len(blocks) * rows // HALF
    held = ps + sum(b.shape[1] for b in before)
    group = nl if nl <= 8 else 4
    return pl.pallas_call(
        functools.partial(transform_kernel, layout, rows),
        grid=(nl // group,),
        in_specs=[whole_block(run) for run in flat]
        + [
            pl.BlockSpec((nl * LANES, group * LANES), lambda i: (0, i)),
            pl.BlockSpec((group, 2 * BLK, nl * HALF), lambda i: (i, 0, 0)),
        ]
        + [pl.BlockSpec((group,) + b.shape[1:], lambda i: (i, 0, 0)) for b in before],
        out_specs=pl.BlockSpec((group, held, BLK * BLK), lambda i: (i, 0, 0)),
        out_shape=jax.ShapeDtypeStruct((nl, held, BLK * BLK), BF16),
        scratch_shapes=[
            pltpu.VMEM((group, nl * HALF, ps * LANES), BF16),
            pltpu.VMEM((ps, HALF, LANES), BF16),
        ],
        compiler_params=pltpu.CompilerParams(vmem_limit_bytes=(18 if nl <= 8 else 36) * MIB),
        name="transform",
    )(*flat, virt, occ, *before)


def prepare_kernel(layout, rows, count, after, nz, k_local, me, pair, *refs):
    g_refs, refs = refs[:count], refs[count:]
    total = sum(map(len, layout))
    runs, refs = refs[:total], refs[total + after :]
    occ, virt, out = refs[:3]
    tables_body(nz, k_local, me, pair, g_refs, occ, virt, *refs[3:8])
    transform_body(runs_of(layout, runs), rows, virt, occ, out, 0, *refs[8:])


def prepare(g_blocks, blocks, rows, me, pair_index, nz, k_local, after):
    nl = pair_index.shape[1]
    nao = len(g_blocks) * g_blocks[0].shape[0] * (g_blocks[0].shape[1] // 8)
    out, scratch = tables_shapes(nao, nl)
    layout = [[length for _, length in block] for block in blocks]
    flat = [run for block in blocks for run, _ in block]
    ps = len(blocks) * rows // HALF
    return pl.pallas_call(
        functools.partial(prepare_kernel, layout, rows, len(g_blocks), len(after), nz, k_local),
        in_specs=[IN_SMEM, IN_SMEM] + [IN_VMEM] * (len(g_blocks) + len(flat)) + [IN_PLACE] * len(after),
        out_specs=[IN_VMEM] * 3,
        out_shape=out + (jax.ShapeDtypeStruct((nl, ps, BLK * BLK), BF16),),
        scratch_shapes=scratch
        + [pltpu.VMEM((nl, nl * HALF, ps * LANES), BF16), pltpu.VMEM((ps, HALF, LANES), BF16)],
        compiler_params=pltpu.CompilerParams(vmem_limit_bytes=27 * MIB),
        name="prepare",
    )(me, pair_index, *g_blocks, *flat, *after)


def reorder_kernel(slab, out, order):
    q, nl, tile = slab.shape
    n = q * nl

    @pl.when(pl.program_id(0) == 0)
    def _():
        for l in range(nl):
            order[l * q : (l + 1) * q, :] = hot(iota((q, n), 1) == iota((q, n), 0) * nl + l)

    at = 0 if out.shape[1] == q else pl.multiple_of(pl.program_id(0) * q, q)
    step = 512
    for t in range(0, tile, step):
        moved = dot(order[...], slab[:, :, t : t + step].reshape(n, step)).astype(BF16)
        for l in range(nl):
            out[l, pl.ds(at, q), t : t + step] = moved[l * q : (l + 1) * q]


def reorder(slab, first, last, parts, space):
    count, nl, tile = slab.shape
    q = 256 // nl
    skip = count * first // parts // q
    steps = count * last // parts // q - skip
    return pl.pallas_call(
        reorder_kernel,
        grid=(steps,),
        in_specs=[pl.BlockSpec((q, nl, tile), lambda i: (skip + i, 0, 0))],
        out_specs=IN_VMEM if space == pltpu.VMEM else pl.BlockSpec((nl, q, tile), lambda i: (0, i, 0)),
        out_shape=space((nl, steps * q, tile), BF16),
        scratch_shapes=[pltpu.VMEM((q * nl, q * nl), BF16)],
        compiler_params=pltpu.CompilerParams(vmem_limit_bytes=16 * MIB),
        name="reorder",
    )(in_hbm(slab))


def pack_kernel(b_in, occ_in, virt_in, out, padded, b_rows, g_occ, g_virt, sems):
    moves = [
        pltpu.make_async_copy(source, to, sems.at[i])
        for i, (source, to) in enumerate(((b_in, b_rows), (occ_in, g_occ), (virt_in, g_virt)))
    ]
    for move in moves:
        move.start()
    for move in moves:
        move.wait()
    per, k_local, _ = b_rows.shape
    for k in range(k_local):
        held = b_rows[:, k, :].astype(F32)
        for p in range(per):
            out[(k * per + p) * HALF : (k * per + p + 1) * HALF, :] = held[p].reshape(HALF, LANES).astype(BF16)
    at = k_local * per * HALF
    strip = g_occ.shape[0]
    for i in range(0, g_occ.shape[1], LANES):
        for ref in (g_occ, g_virt):
            out[at : at + strip, :] = ref[:, i : i + LANES]
            at += strip
    padded[:at, :] = out[...]
    padded[at:, :] = jnp.zeros_like(padded[at:, :])


def pack(b_rows, g_occ, g_virt):
    total = (b_rows.size + 2 * g_occ.size) // LANES
    return pl.pallas_call(
        pack_kernel,
        in_specs=[IN_PLACE] * 3,
        out_specs=[IN_VMEM, IN_VMEM],
        out_shape=(jax.ShapeDtypeStruct((total, LANES), BF16), jax.ShapeDtypeStruct((total + PAD, LANES), BF16)),
        scratch_shapes=[pltpu.VMEM(x.shape, BF16) for x in (b_rows, g_occ, g_virt)] + [pltpu.SemaphoreType.DMA((3,))],
        compiler_params=pltpu.CompilerParams(vmem_limit_bytes=8 * MIB),
        name="pack",
    )(in_hbm(b_rows), in_hbm(g_occ), in_hbm(g_virt))


def stack_kernel(split, nz, after, *refs):
    refs, b_out, g_out = refs[: -2 - after], refs[-2], refs[-1]
    column, side = refs[: nz - 1], refs[nz - 1 :]
    k_local = b_out.shape[0] // len(column)
    rows = split // k_local
    for i, ref in enumerate(column):
        for j in range(k_local):
            b_out[i * k_local + j] = ref[j * rows : (j + 1) * rows, :]
    for i, ref in enumerate(side):
        g_out[i] = ref[split:, :]


def stack(column, side, split, k_local, after):
    one = side[0].shape[0] - split
    return pl.pallas_call(
        functools.partial(stack_kernel, split, len(column) + 1, len(after)),
        in_specs=[IN_VMEM] * (len(column) + len(side)) + [IN_PLACE] * len(after),
        out_specs=[IN_VMEM, IN_VMEM],
        out_shape=(
            jax.ShapeDtypeStruct((len(column) * k_local, split // k_local, LANES), BF16),
            jax.ShapeDtypeStruct((len(side), one, LANES), BF16),
        ),
        compiler_params=pltpu.CompilerParams(vmem_limit_bytes=8 * MIB),
        name="stack",
    )(*column, *side, *after)


def collect_kernel(split, nz, sides, *refs):
    near, side, far, out = refs[:nz], refs[nz : nz + sides], refs[nz + sides : 2 * nz + sides - 1], refs[-1]
    for z, ref in enumerate(near):
        out[z] = ref[split : split + out.shape[1], :]
    for e, ref in enumerate(side):
        out[(e + 1) * nz] = ref[split:, :]
        for z, block in enumerate(far):
            out[(e + 1) * nz + z + 1] = block[e]


def collect(own, column, side, far, split, after):
    nz = len(column) + 1
    return pl.pallas_call(
        functools.partial(collect_kernel, split, nz, len(side)),
        in_specs=[IN_VMEM] * (nz + len(side) + len(far)) + [IN_PLACE] * len(after),
        out_specs=IN_VMEM,
        out_shape=jax.ShapeDtypeStruct((nz * (len(side) + 1), own.shape[0] - split, LANES), BF16),
        compiler_params=pltpu.CompilerParams(vmem_limit_bytes=8 * MIB),
        name="collect",
    )(own, *column, *side, *far, *after)


def contract_kernel(parts, place, *refs):
    slabs, w_refs, out = refs[:parts], refs[parts:-1], refs[-1]
    total = [None] * parts
    for l in range(slabs[0].shape[0]):
        weights = jnp.concatenate([w[l] for w in w_refs], axis=0)
        for i, slab in enumerate(slabs):
            part = dot(slab[l], weights, NT)
            total[i] = part if total[i] is None else total[i] + part
    total = jnp.concatenate(total, axis=0)
    out[...] = dot(place[...], total, NT, precision=lax.Precision.HIGHEST)


def contract(slabs, w_pieces, place):
    parts = len(slabs)
    return pl.pallas_call(
        functools.partial(contract_kernel, parts),
        in_specs=[IN_VMEM] * (1 + parts + len(w_pieces)),
        out_specs=IN_VMEM,
        out_shape=jax.ShapeDtypeStruct((place.shape[0], sum(slab.shape[1] for slab in slabs)), F32),
        compiler_params=pltpu.CompilerParams(vmem_limit_bytes=28 * MIB),
        name="contract",
    )(place, *map(in_vmem, slabs), *w_pieces)


def on_device(na, nz, b_slab, b_rows, g_occ, g_virt, pair_index):
    per, k_local, tile = b_rows.shape
    me_a, me_z = lax.axis_index("aux"), lax.axis_index("pair")
    me = jnp.stack([me_a, me_z]).astype(jnp.int32)
    outer = list(range(0, na, 2))
    rows = per * HALF
    split = k_local * rows

    own, padded = pack(b_rows, g_occ, g_virt)

    side = [swap(own, "aux", na, e) for e in outer[2:]]
    side[0], late = lax.optimization_barrier((side[0], own))
    side = [swap(late, "aux", na, outer[1])] + side
    column = [swap(padded, "pair", nz, d) for d in range(1, nz)]
    slabs = [reorder(b_slab, 0, 2, 4, pltpu.HBM)]
    b_z, g_side = stack(column, side, split, k_local, [in_hbm(slabs[0])])

    b_z, b_slab = lax.optimization_barrier((b_z, b_slab))
    slabs.append(reorder(b_slab, 2, 3, 4, pltpu.HBM))
    g_far = [swap(g_side, "pair", nz, d) for d in range(1, nz)]
    far = [[(swap(b_z, "aux", na, e), b_z.shape[0])] for e in outer[1 : 3 if len(outer) == 4 else None]]
    if len(outer) == 4:
        cut = b_z.shape[0] // 2
        low, high = far[0][0][0][:cut], far[1][0][0][cut:]
        far.append([(swap(low, "aux", na, 4), cut), (swap(high, "aux", na, 2), b_z.shape[0] - cut)])
    close = [block[0][0] for block in far[:2]]
    g_half = collect(own, column, side, g_far, split, [in_hbm(slabs[1])] + (close if len(outer) == 4 else []))
    g_blocks = [g_half, swap(g_half, "aux", na, 1)]
    blocks = [[(own, k_local), (b_z, b_z.shape[0])]] + [[(b, k_local)] + f for b, f in zip(side, far)]
    if len(outer) == 4:
        occ, virt, first = prepare(g_blocks, blocks[:3], rows, me, pair_index, nz, k_local, [])
        pieces = [transform(blocks[3:], rows, occ, virt, [first])]
    else:
        occ, virt = make_tables(g_blocks, me, pair_index, nz, k_local)
        pieces = [transform(blocks[i : i + 2], rows, occ, virt) for i in range(0, len(outer), 2)]
    pieces[-1], b_slab = lax.optimization_barrier((pieces[-1], b_slab))
    others = [swap(w, "aux", na, 1) for w in pieces]

    count = na * per
    at = jnp.arange(count, dtype=jnp.int32)
    block = at // per
    target = (me_a ^ (2 * (block % (na // 2)) + block // (na // 2))) * per + at % per
    place = (target[None, :] == at[:, None]).astype(F32)
    slabs.append(reorder(b_slab, 3, 4, 4, pltpu.VMEM))
    return contract(slabs, pieces + others, place).T


def solution(mesh):
    placed = (
        P(("aux", "pair"), None, None),
        P("aux", "pair", None),
        P(("aux", "pair"), None),
        P(("aux", "pair"), None),
        P(),
    )
    return jax.shard_map(
        functools.partial(on_device, mesh.shape["aux"], mesh.shape["pair"]),
        mesh=mesh,
        in_specs=placed,
        out_specs=P(("aux", "pair"), None),
        check_vma=False,
    )
```
